32 devices in a mesh: layer: 2 (over x), row: 4 (over y, core), col: 4 (over z).
Axes of the slice: x: 2, y: 2, z: 4, core: 2. Of those that a mesh axis runs over, the one named last changes fastest.
Arguments:
- lower_inverse: bfloat16 [2, 4096, 4096], P('layer', 'row', 'col')
- upper_inverse: bfloat16 [2, 4096, 4096], P('layer', 'col', 'row')
- lower_coupling: bfloat16 [2, 4096, 8192], P('layer', 'row', 'col'), may hold values from -0.0625 to 0.0625
- upper_coupling: bfloat16 [2, 4096, 8192], P('layer', 'row', 'col'), may hold values from -0.0625 to 0.0625
- separator_lower: bfloat16 [8192, 8192], P(('layer', 'row'), 'col')
- separator_upper: bfloat16 [8192, 8192], P('col', ('layer', 'row'))
- subtree_rhs: float32 [2, 4096, 512], P('layer', 'col', 'row'), may hold values from -6 to 6
- separator_rhs: float32 [8192, 512], P('col', ('layer', 'row')), may hold values from -6 to 6
- column_counts: int32 [2], P('layer'), may hold values from 1024 to 4096, as said below
Outputs:
- subtree_solution: float32 [2, 4096, 512], P('layer', 'col', 'row')
- separator_solution: float32 [8192, 512], P('col', ('layer', 'row'))
The draws below stay inside these ranges and needn't reach their ends.
Inputs may be any that keep to these rules, and one draw needn't show every extreme that they name: `column_counts`: each count is a multiple of 128.
All inputs are finite; a program needn't handle non-finite values.
Results may differ from the reference program's by a relative error of at most 0.019.
Values may be sent and summed in bfloat16 or wider, within the bound.
No kernel may reach another device: no remote copies, remote signals or barrier semaphores. Data moves between devices by JAX's collectives and lax.ppermute only.
A program may use at most 64 MiB of HBM per device.

```python
import math
import jax
import jax.numpy as jnp

NS = 4096
NSEP = 8192
R = 512
LAYERS = 2


def triangle(key, order, lower):
    noise = jax.random.normal(key, (order, order), jnp.float32) * (0.5 / math.sqrt(order))
    places = jnp.arange(order)
    if lower:
        inside = places[:, None] > places[None, :]
    else:
        inside = places[:, None] < places[None, :]
    return jnp.eye(order, dtype=jnp.float32) + jnp.where(inside, noise, 0.0)


def draw_lower_inverse(key, part):
    keyset = jax.random.split(jax.random.fold_in(key, 11), LAYERS)
    return jax.vmap(lambda single: triangle(single, NS, True))(keyset).astype(jnp.bfloat16)


def draw_upper_inverse(key, part):
    keyset = jax.random.split(jax.random.fold_in(key, 12), LAYERS)
    return jax.vmap(lambda single: triangle(single, NS, False))(keyset).astype(jnp.bfloat16)


def draw_separator_lower(key, part):
    return triangle(jax.random.fold_in(key, 13), NSEP, True).astype(jnp.bfloat16)


def draw_separator_upper(key, part):
    return triangle(jax.random.fold_in(key, 14), NSEP, False).astype(jnp.bfloat16)


def draw_column_counts(key, part):
    lowest = max(1, NS // 512)
    tiles = jax.random.randint(jax.random.fold_in(key, 15), (LAYERS,), lowest, NS // 128 + 1, dtype=jnp.int32)
    order = jax.random.permutation(jax.random.fold_in(key, 16), LAYERS)
    tiles = tiles.at[order[0]].set(NS // 128)
    return 128 * tiles


def steps_of(key, dims, shards, smallest, top_value):
    def one(dim, blocks):
        draws = jax.random.uniform(jax.random.fold_in(jax.random.fold_in(key, 6), dim), (blocks,), jnp.float32, smallest / len(shards), top_value / len(shards))
        return jnp.repeat(jnp.exp(draws), dims[dim] // blocks).reshape((-1,) + (1,) * (len(dims) - dim - 1))

    level = one(*shards[0])
    for cut in shards[1:]:
        level = level * one(*cut)
    return level


def normal_values(rng, extent, deviation, most, cuts=(), kind=jnp.bfloat16):
    result = deviation * jax.random.normal(rng, extent, jnp.float32)
    if cuts:
        result = result * steps_of(rng, extent, cuts, -0.22, 0.18)
    return jnp.clip(result, -most, most).astype(kind)


def setup_inputs(seed: int = 0) -> dict:
    arg_keys = jax.random.split(jax.random.key(seed), 10)
    lower_inverse = draw_lower_inverse(jax.random.fold_in(arg_keys[9], 71), 0)
    upper_inverse = draw_upper_inverse(jax.random.fold_in(arg_keys[9], 71), 0)
    lower_coupling = normal_values(arg_keys[2], (LAYERS, NS, NSEP), (NS * LAYERS) ** -0.5, 0.0625, ((0, 2), (1, 4), (2, 4)))
    upper_coupling = normal_values(arg_keys[3], (LAYERS, NS, NSEP), NSEP ** -0.5, 0.0625, ((0, 2), (1, 4), (2, 4)))
    separator_lower = draw_separator_lower(jax.random.fold_in(arg_keys[9], 71), 0)
    separator_upper = draw_separator_upper(jax.random.fold_in(arg_keys[9], 71), 0)
    subtree_rhs = normal_values(arg_keys[6], (LAYERS, NS, R), 1.0, 6.0, ((0, 2), (1, 4), (2, 4)), jnp.float32)
    separator_rhs = normal_values(arg_keys[7], (NSEP, R), 1.0, 6.0, ((0, 4), (1, 8)), jnp.float32)
    column_counts = draw_column_counts(jax.random.fold_in(arg_keys[9], 71), 0)
    return dict(lower_inverse=lower_inverse, upper_inverse=upper_inverse, lower_coupling=lower_coupling, upper_coupling=upper_coupling, separator_lower=separator_lower, separator_upper=separator_upper, subtree_rhs=subtree_rhs, separator_rhs=separator_rhs, column_counts=column_counts)


def reference(lower_inverse, upper_inverse, lower_coupling, upper_coupling, separator_lower, separator_upper, subtree_rhs, separator_rhs, column_counts):
    positions = jnp.arange(NS, dtype=jnp.int32)
    masks = (positions[None, :] < column_counts[:, None]).astype(jnp.float32)
    forwards = []
    update = jnp.zeros((NSEP, R), jnp.float32)
    for member in range(LAYERS):
        keeper = masks[member][:, None]
        masked = (subtree_rhs[member] * keeper).astype(jnp.bfloat16)
        solved = jnp.dot(lower_inverse[member], masked, preferred_element_type=jnp.float32) * keeper
        forwards.append(solved)
        update = update + jnp.dot(lower_coupling[member].T, solved.astype(jnp.bfloat16), preferred_element_type=jnp.float32)
    reduced = (separator_rhs - update).astype(jnp.bfloat16)
    middle = jnp.dot(separator_lower, reduced, preferred_element_type=jnp.float32).astype(jnp.bfloat16)
    separator_solution = jnp.dot(separator_upper, middle, preferred_element_type=jnp.float32)
    spread = separator_solution.astype(jnp.bfloat16)
    results = []
    for member in range(LAYERS):
        keeper = masks[member][:, None]
        coupled = jnp.dot(upper_coupling[member], spread, preferred_element_type=jnp.float32)
        interior = ((forwards[member] - coupled) * keeper).astype(jnp.bfloat16)
        results.append(jnp.dot(upper_inverse[member], interior, preferred_element_type=jnp.float32) * keeper)
    return jnp.stack(results), separator_solution
```

```python
import jax
import jax.numpy as jnp
from jax import lax
from jax.sharding import PartitionSpec as P

F32 = jnp.float32
BF16 = jnp.bfloat16


def pick(array, index):
    return lax.dynamic_index_in_dim(array, index, 0, keepdims=False)


def place(parts):
    out = jnp.zeros((len(parts),) + parts[0][1].shape, parts[0][1].dtype)
    for index, block in parts:
        out = lax.dynamic_update_index_in_dim(out, block, index, 0)
    return out


def dot_nt(a, b):
    return lax.dot_general(a, b, (((1,), (1,)), ((), ())), preferred_element_type=F32)


def solution(mesh):
    layers, rows, cols = (mesh.shape[name] for name in ("layer", "row", "col"))
    pair = 2 if rows % 2 == 0 else 1
    high = rows // pair
    groups = layers * high

    def send_col(block, step):
        return lax.ppermute(block, "col", [(i, (i + step) % cols) for i in range(cols)])

    def send_high(block, step):
        return lax.ppermute(
            block,
            "row",
            [(i, (i // pair + step) % high * pair + i % pair) for i in range(rows)],
        )

    def send_pair(block):
        return lax.ppermute(block, "row", [(i, i ^ 1) for i in range(rows)])

    def send_group(block, step):
        return lax.ppermute(
            block,
            ("layer", "row"),
            [
                (i, (i // pair + step) % groups * pair + i % pair)
                for i in range(layers * rows)
            ],
        )

    def scatter(part, me, size, send):
        total = pick(part, me)
        low = part.astype(BF16)
        got = [send(pick(low, (me + k) % size), k) for k in range(1, size)]
        for block in got:
            total = total + block.astype(F32)
        return total

    def gather(block, me, size, send):
        return place(
            [(me, block)] + [((me - k) % size, send(block, k)) for k in range(1, size)]
        )

    def pair_scatter(part, core):
        if pair == 1:
            return part[:, 0]
        mine = lax.dynamic_index_in_dim(part, core, 1, keepdims=False)
        other = lax.dynamic_index_in_dim(part, 1 - core, 1, keepdims=False)
        return mine + send_pair(other.astype(BF16)).astype(F32)

    def pair_gather(block, core):
        if pair == 1:
            return block[:, None]
        out = jnp.zeros((block.shape[0], pair) + block.shape[1:], block.dtype)
        out = lax.dynamic_update_index_in_dim(out, block, core, 1)
        return lax.dynamic_update_index_in_dim(out, send_pair(block), 1 - core, 1)

    def shards(
        lower_inverse,
        upper_inverse,
        lower_coupling,
        upper_coupling,
        separator_lower,
        separator_upper,
        subtree_rhs,
        separator_rhs,
        column_counts,
    ):
        limit = column_counts[0]
        row_count = lower_inverse.shape[1]
        col_count = lower_inverse.shape[2]
        sep_count, width = separator_rhs.shape
        chunks = 2 if width % 32 == 0 else 1
        part = width // chunks
        total = layers * rows * part
        layer, row, col = (lax.axis_index(name) for name in ("layer", "row", "col"))
        core, up = row % pair, row // pair
        group = layer * high + up
        col_mask = (col * col_count + lax.iota(jnp.int32, col_count) < limit).astype(F32)
        row_mask = (row * row_count + lax.iota(jnp.int32, row_count) < limit).astype(F32)

        def col_scatter(x):
            return scatter(x.reshape(cols, -1, x.shape[1]), col, cols, send_col)

        def col_gather(x):
            return gather(x, col, cols, send_col).reshape(total, -1)

        def all_scatter(x):
            n = x.shape[1]
            mine = pair_scatter(x.reshape(groups, pair, part, n), core)
            return scatter(mine, group, groups, send_group)

        def all_gather(x):
            mine = gather(x, group, groups, send_group)
            return pair_gather(mine, core).reshape(total, -1)

        def row_gather(x):
            return pair_gather(gather(x, up, high, send_high), core).reshape(total, -1)

        def row_scatter(x):
            n = x.shape[1]
            mine = pair_scatter(x.reshape(high, pair, -1, n), core)
            return scatter(mine, up, high, send_high)

        given = (subtree_rhs[0] * col_mask[:, None]).astype(BF16).T
        given = given.reshape(layers, chunks, part, col_count)
        sep_given = separator_rhs.T.reshape(chunks, part, sep_count)

        solved, middles = [], []
        for h in range(chunks):
            masked = row_gather(given[:, h].reshape(layers * part, col_count))
            forward = col_scatter(dot_nt(masked, lower_inverse[0])) * row_mask
            update = jnp.dot(
                col_gather(forward.astype(BF16)),
                lower_coupling[0],
                preferred_element_type=F32,
            )
            reduced = all_gather((sep_given[h] - all_scatter(update)).astype(BF16))
            middle = col_gather(col_scatter(dot_nt(reduced, separator_lower)).astype(BF16))
            spread = all_scatter(dot_nt(middle, separator_upper))
            coupled = col_scatter(
                dot_nt(all_gather(spread.astype(BF16)), upper_coupling[0])
            )
            interior = col_gather(((forward - coupled) * row_mask).astype(BF16))
            back = row_scatter(dot_nt(interior, upper_inverse[0])) * col_mask
            middles.append(spread)
            solved.append(back.reshape(layers, 1, part, col_count))
        out = jnp.concatenate(solved, axis=1).reshape(layers * width, col_count).T
        return out[None], jnp.concatenate(middles, axis=0).T

    placed = (
        P("layer", "row", "col"),
        P("layer", "col", "row"),
        P("layer", "row", "col"),
        P("layer", "row", "col"),
        P(("layer", "row"), "col"),
        P("col", ("layer", "row")),
        P("layer", "col", "row"),
        P("col", ("layer", "row")),
        P("layer"),
    )
    return jax.shard_map(
        shards,
        mesh=mesh,
        in_specs=placed,
        out_specs=(P("layer", "col", "row"), P("col", ("layer", "row"))),
        check_vma=False,
    )
```

```python
import jax
import jax.numpy as jnp
from jax import lax
from jax.sharding import PartitionSpec as P

F32 = jnp.float32
BF16 = jnp.bfloat16


def pick(array, index):
    return lax.dynamic_index_in_dim(array, index, 0, keepdims=False)


def place(parts):
    out = jnp.zeros((len(parts),) + parts[0][1].shape, parts[0][1].dtype)
    for index, block in parts:
        out = lax.dynamic_update_index_in_dim(out, block, index, 0)
    return out


def dot_nt(a, b):
    return lax.dot_general(a, b, (((1,), (1,)), ((), ())), preferred_element_type=F32)


def solution(mesh):
    layers, rows, cols = (mesh.shape[name] for name in ("layer", "row", "col"))
    pair = 2 if rows % 2 == 0 else 1
    high = rows // pair
    groups = layers * high

    def send_col(block, step):
        return lax.ppermute(block, "col", [(i, (i + step) % cols) for i in range(cols)])

    def send_high(block, step):
        return lax.ppermute(
            block,
            "row",
            [(i, (i // pair + step) % high * pair + i % pair) for i in range(rows)],
        )

    def send_pair(block):
        return lax.ppermute(block, "row", [(i, i ^ 1) for i in range(rows)])

    def send_group(block, step):
        return lax.ppermute(
            block,
            ("layer", "row"),
            [
                (i, (i // pair + step) % groups * pair + i % pair)
                for i in range(layers * rows)
            ],
        )

    def scatter(part, me, size, send):
        total = pick(part, me)
        low = part.astype(BF16)
        got = [send(pick(low, (me + k) % size), k) for k in range(1, size)]
        for block in got:
            total = total + block.astype(F32)
        return total

    def gather(block, me, size, send):
        return place(
            [(me, block)] + [((me - k) % size, send(block, k)) for k in range(1, size)]
        )

    def swap_col(block, bits):
        return lax.ppermute(block, "col", [(i, i ^ bits) for i in range(cols)])

    def line_scatter(part, me):
        low = part.astype(BF16)
        far = swap_col(pick(low, me ^ 2), 1)
        near = swap_col(pick(low, me ^ 1), 1)
        across = swap_col((pick(part, me ^ 3) + far.astype(F32)).astype(BF16), 3)
        return pick(part, me) + near.astype(F32) + across.astype(F32)

    def line_gather(block, me):
        across = swap_col(block, 3)
        near = swap_col(block, 1)
        far = swap_col(across, 1)
        return place([(me, block), (me ^ 1, near), (me ^ 3, across), (me ^ 2, far)])

    def pair_scatter(part, core):
        if pair == 1:
            return part[:, 0]
        mine = lax.dynamic_index_in_dim(part, core, 1, keepdims=False)
        other = lax.dynamic_index_in_dim(part, 1 - core, 1, keepdims=False)
        return mine + send_pair(other.astype(BF16)).astype(F32)

    def pair_gather(block, core):
        if pair == 1:
            return block[:, None]
        out = jnp.zeros((block.shape[0], pair) + block.shape[1:], block.dtype)
        out = lax.dynamic_update_index_in_dim(out, block, core, 1)
        return lax.dynamic_update_index_in_dim(out, send_pair(block), 1 - core, 1)

    def shards(
        lower_inverse,
        upper_inverse,
        lower_coupling,
        upper_coupling,
        separator_lower,
        separator_upper,
        subtree_rhs,
        separator_rhs,
        column_counts,
    ):
        limit = column_counts[0]
        row_count = lower_inverse.shape[1]
        col_count = lower_inverse.shape[2]
        sep_count, width = separator_rhs.shape
        chunks = 2 if width % 32 == 0 else 1
        part = width // chunks
        total = layers * rows * part
        layer, row, col = (lax.axis_index(name) for name in ("layer", "row", "col"))
        core, up = row % pair, row // pair
        group = layer * high + up
        col_mask = (col * col_count + lax.iota(jnp.int32, col_count) < limit).astype(F32)
        row_mask = (row * row_count + lax.iota(jnp.int32, row_count) < limit).astype(F32)

        def col_scatter(x):
            pieces = x.reshape(cols, -1, x.shape[1])
            if cols == 4:
                return line_scatter(pieces, col)
            return scatter(pieces, col, cols, send_col)

        def col_gather(x):
            if cols == 4:
                return line_gather(x, col).reshape(total, -1)
            return gather(x, col, cols, send_col).reshape(total, -1)

        def all_scatter(x):
            n = x.shape[1]
            mine = pair_scatter(x.reshape(groups, pair, part, n), core)
            return scatter(mine, group, groups, send_group)

        def all_gather(x):
            mine = gather(x, group, groups, send_group)
            return pair_gather(mine, core).reshape(total, -1)

        def row_gather(x):
            return pair_gather(gather(x, up, high, send_high), core).reshape(total, -1)

        def row_scatter(x):
            n = x.shape[1]
            mine = pair_scatter(x.reshape(high, pair, -1, n), core)
            return scatter(mine, up, high, send_high)

        given = (subtree_rhs[0] * col_mask[:, None]).astype(BF16).T
        given = given.reshape(layers, chunks, part, col_count)
        sep_given = separator_rhs.T.reshape(chunks, part, sep_count)

        solved, middles = [], []
        for h in range(chunks):
            masked = row_gather(given[:, h].reshape(layers * part, col_count))
            forward = col_scatter(dot_nt(masked, lower_inverse[0])) * row_mask
            update = jnp.dot(
                col_gather(forward.astype(BF16)),
                lower_coupling[0],
                preferred_element_type=F32,
            )
            reduced = all_gather((sep_given[h] - all_scatter(update)).astype(BF16))
            middle = col_gather(col_scatter(dot_nt(reduced, separator_lower)).astype(BF16))
            spread = all_scatter(dot_nt(middle, separator_upper))
            coupled = col_scatter(
                dot_nt(all_gather(spread.astype(BF16)), upper_coupling[0])
            )
            interior = col_gather(((forward - coupled) * row_mask).astype(BF16))
            back = row_scatter(dot_nt(interior, upper_inverse[0])) * col_mask
            middles.append(spread)
            solved.append(back.reshape(layers, 1, part, col_count))
        out = jnp.concatenate(solved, axis=1).reshape(layers * width, col_count).T
        return out[None], jnp.concatenate(middles, axis=0).T

    placed = (
        P("layer", "row", "col"),
        P("layer", "col", "row"),
        P("layer", "row", "col"),
        P("layer", "row", "col"),
        P(("layer", "row"), "col"),
        P("col", ("layer", "row")),
        P("layer", "col", "row"),
        P("col", ("layer", "row")),
        P("layer"),
    )
    return jax.shard_map(
        shards,
        mesh=mesh,
        in_specs=placed,
        out_specs=(P("layer", "col", "row"), P("col", ("layer", "row"))),
        check_vma=False,
    )
```

```python
import jax
import jax.numpy as jnp
from jax import lax
from jax.sharding import PartitionSpec as P

F32 = jnp.float32
BF16 = jnp.bfloat16


def pick(array, index):
    return lax.dynamic_index_in_dim(array, index, 0, keepdims=False)


def place(parts):
    out = jnp.zeros((len(parts),) + parts[0][1].shape, parts[0][1].dtype)
    for index, block in parts:
        out = lax.dynamic_update_index_in_dim(out, block, index, 0)
    return out


WAITS = (1, None, None, None)


def alone(steps):
    try:
        event = next(steps)
        while True:
            event = steps.send(None)
    except StopIteration as end:
        return end.value


def staggered(first, second):
    ends = {}
    events = {}

    def step(name, chunk, wait=None):
        try:
            events[name] = chunk.send(wait) if name in events else next(chunk)
        except StopIteration as end:
            ends[name] = end.value
            return None
        return events[name]

    step("a", first)
    step("b", second)
    last = None
    for _ in range(4):
        last = step("a", first)
    ahead, behind = ("b", second), ("a", first)
    for stage in range(5):
        seen = [last]
        for wait in WAITS:
            while wait is not None and len(seen) <= wait:
                seen.append(None if behind[0] in ends else step(*behind))
            got = step(*ahead, None if wait is None else seen[wait])
        last = got
        while len(seen) < 6:
            seen.append(None if behind[0] in ends else step(*behind))
        ahead, behind = behind, ahead
    for name, chunk in (("a", first), ("b", second)):
        while name not in ends:
            step(name, chunk)
    return ends["a"], ends["b"]


def dot_nt(a, b):
    return lax.dot_general(a, b, (((1,), (1,)), ((), ())), preferred_element_type=F32)


def solution(mesh):
    layers, rows, cols = (mesh.shape[name] for name in ("layer", "row", "col"))
    pair = 2 if rows % 2 == 0 else 1
    high = rows // pair
    groups = layers * high

    def send_col(block, step):
        return lax.ppermute(block, "col", [(i, (i + step) % cols) for i in range(cols)])

    def send_high(block, step):
        return lax.ppermute(
            block,
            "row",
            [(i, (i // pair + step) % high * pair + i % pair) for i in range(rows)],
        )

    def send_pair(block):
        return lax.ppermute(block, "row", [(i, i ^ 1) for i in range(rows)])

    def send_group(block, step):
        return lax.ppermute(
            block,
            ("layer", "row"),
            [
                (i, (i // pair + step) % groups * pair + i % pair)
                for i in range(layers * rows)
            ],
        )

    def scatter(part, me, size, send):
        total = pick(part, me)
        low = part.astype(BF16)
        got = [send(pick(low, (me + k) % size), k) for k in range(1, size)]
        for block in got:
            total = total + block.astype(F32)
        return total

    def gather(block, me, size, send):
        parts = [(me, block)]
        parts += [((me - k) % size, send(block, k)) for k in range(1, size)]
        return place(parts), parts[-1][1]

    def swap_col(block, bits):
        return lax.ppermute(block, "col", [(i, i ^ bits) for i in range(cols)])

    def after(block, event):
        if event is None:
            return block
        row = event.reshape(-1, event.shape[-1])[:1, : block.shape[-1]].astype(F32)
        return block + jnp.where((row < 0) & (row > 0), row, 0).astype(block.dtype)

    def line_scatter(part, me, event):
        low = part.astype(BF16)
        far = swap_col(after(pick(low, me ^ 2), event), 1)
        near = swap_col(after(pick(low, me ^ 1), event), 1)
        event = yield far
        across = pick(part, me ^ 3) + far.astype(F32)
        across = swap_col(after(across, event).astype(BF16), 3)
        event = yield across
        return pick(part, me) + near.astype(F32) + across.astype(F32), event

    def line_gather(block, me, event):
        block = after(block, event)
        across = swap_col(block, 3)
        near = swap_col(block, 1)
        event = yield across
        far = swap_col(after(across, event), 1)
        event = yield far
        return place([(me, block), (me ^ 1, near), (me ^ 3, across), (me ^ 2, far)]), event

    def pair_scatter(part, core):
        if pair == 1:
            return part[:, 0], part
        mine = lax.dynamic_index_in_dim(part, core, 1, keepdims=False)
        other = lax.dynamic_index_in_dim(part, 1 - core, 1, keepdims=False)
        got = send_pair(other.astype(BF16))
        return mine + got.astype(F32), got

    def pair_gather(block, core):
        if pair == 1:
            return block[:, None], block
        got = send_pair(block)
        out = jnp.zeros((block.shape[0], pair) + block.shape[1:], block.dtype)
        out = lax.dynamic_update_index_in_dim(out, block, core, 1)
        return lax.dynamic_update_index_in_dim(out, got, 1 - core, 1), got

    def shards(
        lower_inverse,
        upper_inverse,
        lower_coupling,
        upper_coupling,
        separator_lower,
        separator_upper,
        subtree_rhs,
        separator_rhs,
        column_counts,
    ):
        limit = column_counts[0]
        row_count = lower_inverse.shape[1]
        col_count = lower_inverse.shape[2]
        sep_count, width = separator_rhs.shape
        chunks = 2 if width % 32 == 0 else 1
        part = width // chunks
        total = layers * rows * part
        layer, row, col = (lax.axis_index(name) for name in ("layer", "row", "col"))
        core, up = row % pair, row // pair
        group = layer * high + up
        col_mask = (col * col_count + lax.iota(jnp.int32, col_count) < limit).astype(F32)
        row_mask = (row * row_count + lax.iota(jnp.int32, row_count) < limit).astype(F32)

        def col_scatter(x, event):
            pieces = x.reshape(cols, -1, x.shape[1])
            if cols == 4:
                return (yield from line_scatter(pieces, col, event))
            return scatter(pieces, col, cols, send_col), None

        def col_gather(x, event):
            if cols == 4:
                out, event = yield from line_gather(x, col, event)
            else:
                out = gather(x, col, cols, send_col)[0]
            return out.reshape(total, -1), event

        def all_scatter(x):
            n = x.shape[1]
            mine, got = pair_scatter(x.reshape(groups, pair, part, n), core)
            yield got
            out = scatter(mine, group, groups, send_group)
            yield out
            return out

        def all_gather(x):
            mine, got = gather(x, group, groups, send_group)
            yield got
            out, got = pair_gather(mine, core)
            yield got
            return out.reshape(total, -1)

        def row_gather(x):
            mine = gather(x, up, high, send_high)[0]
            return pair_gather(mine, core)[0].reshape(total, -1)

        def row_scatter(x):
            n = x.shape[1]
            mine = pair_scatter(x.reshape(high, pair, -1, n), core)[0]
            return scatter(mine, up, high, send_high)

        given = (subtree_rhs[0] * col_mask[:, None]).astype(BF16).T
        given = given.reshape(layers, chunks, part, col_count)
        sep_given = separator_rhs.T.reshape(chunks, part, sep_count)

        def chunk(h):
            masked = row_gather(given[:, h].reshape(layers * part, col_count))
            event = yield None
            forward, event = yield from col_scatter(dot_nt(masked, lower_inverse[0]), event)
            forward = lax.optimization_barrier(forward * row_mask)
            low, _ = yield from col_gather(forward.astype(BF16), event)
            update = jnp.dot(low, lower_coupling[0], preferred_element_type=F32)
            share = yield from all_scatter(update)
            reduced = yield from all_gather((sep_given[h] - share).astype(BF16))
            event = yield None
            middle, event = yield from col_scatter(dot_nt(reduced, separator_lower), event)
            middle, _ = yield from col_gather(middle.astype(BF16), event)
            spread = yield from all_scatter(dot_nt(middle, separator_upper))
            got = yield from all_gather(spread.astype(BF16))
            event = yield None
            coupled, event = yield from col_scatter(dot_nt(got, upper_coupling[0]), event)
            interior = ((forward - coupled) * row_mask).astype(BF16)
            interior, _ = yield from col_gather(interior, event)
            back = row_scatter(dot_nt(interior, upper_inverse[0])) * col_mask
            return back.reshape(layers, 1, part, col_count), spread

        solved, middles = zip(
            *(
                staggered(chunk(0), chunk(1))
                if chunks == 2
                else [alone(chunk(h)) for h in range(chunks)]
            )
        )
        out = jnp.concatenate(solved, axis=1).reshape(layers * width, col_count).T
        return out[None], jnp.concatenate(middles, axis=0).T

    placed = (
        P("layer", "row", "col"),
        P("layer", "col", "row"),
        P("layer", "row", "col"),
        P("layer", "row", "col"),
        P(("layer", "row"), "col"),
        P("col", ("layer", "row")),
        P("layer", "col", "row"),
        P("col", ("layer", "row")),
        P("layer"),
    )
    return jax.shard_map(
        shards,
        mesh=mesh,
        in_specs=placed,
        out_specs=(P("layer", "col", "row"), P("col", ("layer", "row"))),
        check_vma=False,
    )
```

```python
import jax
import jax.numpy as jnp
from jax import lax
from jax.sharding import PartitionSpec as P

F32 = jnp.float32
BF16 = jnp.bfloat16


def pick(array, index):
    return lax.dynamic_index_in_dim(array, index, 0, keepdims=False)


def place(parts):
    out = jnp.zeros((len(parts),) + parts[0][1].shape, parts[0][1].dtype)
    for index, block in parts:
        out = lax.dynamic_update_index_in_dim(out, block, index, 0)
    return out


WAITS = (1, None, None, None)


def alone(steps):
    try:
        event = next(steps)
        while True:
            event = steps.send(None)
    except StopIteration as end:
        return end.value


def staggered(first, second):
    ends = {}
    events = {}

    def step(name, chunk, wait=None):
        try:
            events[name] = chunk.send(wait) if name in events else next(chunk)
        except StopIteration as end:
            ends[name] = end.value
            return None
        return events[name]

    step("a", first)
    step("b", second)
    last = None
    for _ in range(4):
        last = step("a", first)
    ahead, behind = ("b", second), ("a", first)
    for stage in range(5):
        seen = [last]
        for wait in WAITS:
            while wait is not None and len(seen) <= wait:
                seen.append(None if behind[0] in ends else step(*behind))
            got = step(*ahead, None if wait is None else seen[wait])
        last = got
        while len(seen) < 6:
            seen.append(None if behind[0] in ends else step(*behind))
        ahead, behind = behind, ahead
    for name, chunk in (("a", first), ("b", second)):
        while name not in ends:
            step(name, chunk)
    return ends["a"], ends["b"]


def dot_nt(a, b):
    return lax.dot_general(a, b, (((1,), (1,)), ((), ())), preferred_element_type=F32)


def solution(mesh):
    layers, rows, cols = (mesh.shape[name] for name in ("layer", "row", "col"))
    pair = 2 if rows % 2 == 0 else 1
    high = rows // pair
    groups = layers * high

    def send_col(block, step):
        return lax.ppermute(block, "col", [(i, i ^ step) for i in range(cols)])

    def send_high(block, step):
        return lax.ppermute(
            block,
            "row",
            [(i, i ^ (step * pair)) for i in range(rows)],
        )

    def send_pair(block):
        return lax.ppermute(block, "row", [(i, i ^ 1) for i in range(rows)])

    def send_group(block, step):
        return lax.ppermute(
            block,
            ("layer", "row"),
            [(i, i ^ (step * pair)) for i in range(layers * rows)],
        )

    def scatter(part, me, size, send):
        total = pick(part, me)
        low = part.astype(BF16)
        got = [send(pick(low, me ^ d), d) for d in range(size - 1, 0, -1)]
        for block in got:
            total = total + block.astype(F32)
        return total

    def gather(block, me, size, send):
        parts = [(me, block)]
        parts += [(me ^ d, send(block, d)) for d in range(size - 1, 0, -1)]
        return place(parts), parts[-1][1]

    def swap_col(block, bits):
        return lax.ppermute(block, "col", [(i, i ^ bits) for i in range(cols)])

    def after(block, event):
        if event is None:
            return block
        row = event.reshape(-1, event.shape[-1])[:1, : block.shape[-1]].astype(F32)
        return block + jnp.where((row < 0) & (row > 0), row, 0).astype(block.dtype)

    def line_scatter(part, me, event):
        low = part.astype(BF16)
        far = swap_col(after(pick(low, me ^ 2), event), 1)
        near = swap_col(after(pick(low, me ^ 1), event), 1)
        event = yield far
        across = pick(part, me ^ 3) + far.astype(F32)
        across = swap_col(after(across, event).astype(BF16), 3)
        event = yield across
        return pick(part, me) + near.astype(F32) + across.astype(F32), event

    def line_gather(block, me, event):
        block = after(block, event)
        across = swap_col(block, 3)
        near = swap_col(block, 1)
        event = yield across
        far = swap_col(after(across, event), 1)
        event = yield far
        return place([(me, block), (me ^ 1, near), (me ^ 3, across), (me ^ 2, far)]), event

    def pair_scatter(part, core):
        if pair == 1:
            return part[:, 0], part
        mine = lax.dynamic_index_in_dim(part, core, 1, keepdims=False)
        other = lax.dynamic_index_in_dim(part, 1 - core, 1, keepdims=False)
        got = send_pair(other.astype(BF16))
        return mine + got.astype(F32), got

    def pair_gather(block, core):
        if pair == 1:
            return block[:, None], block
        got = send_pair(block)
        out = jnp.zeros((block.shape[0], pair) + block.shape[1:], block.dtype)
        out = lax.dynamic_update_index_in_dim(out, block, core, 1)
        return lax.dynamic_update_index_in_dim(out, got, 1 - core, 1), got

    def shards(
        lower_inverse,
        upper_inverse,
        lower_coupling,
        upper_coupling,
        separator_lower,
        separator_upper,
        subtree_rhs,
        separator_rhs,
        column_counts,
    ):
        limit = column_counts[0]
        row_count = lower_inverse.shape[1]
        col_count = lower_inverse.shape[2]
        sep_count, width = separator_rhs.shape
        chunks = 2 if width % 32 == 0 else 1
        part = width // chunks
        total = layers * rows * part
        layer, row, col = (lax.axis_index(name) for name in ("layer", "row", "col"))
        core, up = row % pair, row // pair
        group = layer * high + up
        col_mask = (col * col_count + lax.iota(jnp.int32, col_count) < limit).astype(F32)
        row_mask = (row * row_count + lax.iota(jnp.int32, row_count) < limit).astype(F32)

        def col_scatter(x, event):
            pieces = x.reshape(cols, -1, x.shape[1])
            if cols == 4:
                return (yield from line_scatter(pieces, col, event))
            return scatter(pieces, col, cols, send_col), None

        def col_gather(x, event):
            if cols == 4:
                out, event = yield from line_gather(x, col, event)
            else:
                out = gather(x, col, cols, send_col)[0]
            return out.reshape(total, -1), event

        def all_scatter(x):
            n = x.shape[1]
            mine, got = pair_scatter(x.reshape(groups, pair, part, n), core)
            yield got
            out = scatter(mine, group, groups, send_group)
            yield out
            return out

        def all_gather(x):
            mine, got = gather(x, group, groups, send_group)
            yield got
            out, got = pair_gather(mine, core)
            yield got
            return out.reshape(total, -1)

        def row_gather(x):
            mine = gather(x, up, high, send_high)[0]
            return pair_gather(mine, core)[0].reshape(total, -1)

        def row_scatter(x):
            n = x.shape[1]
            mine = pair_scatter(x.reshape(high, pair, -1, n), core)[0]
            return scatter(mine, up, high, send_high)

        given = (subtree_rhs[0] * col_mask[:, None]).astype(BF16).T
        given = given.reshape(layers, chunks, part, col_count)
        sep_given = separator_rhs.T.reshape(chunks, part, sep_count)

        def chunk(h):
            masked = row_gather(given[:, h].reshape(layers * part, col_count))
            event = yield None
            forward, event = yield from col_scatter(dot_nt(masked, lower_inverse[0]), event)
            forward = lax.optimization_barrier(forward * row_mask)
            low, _ = yield from col_gather(forward.astype(BF16), event)
            update = jnp.dot(low, lower_coupling[0], preferred_element_type=F32)
            share = yield from all_scatter(update)
            reduced = yield from all_gather((sep_given[h] - share).astype(BF16))
            event = yield None
            middle, event = yield from col_scatter(dot_nt(reduced, separator_lower), event)
            middle, _ = yield from col_gather(middle.astype(BF16), event)
            spread = yield from all_scatter(dot_nt(middle, separator_upper))
            got = yield from all_gather(spread.astype(BF16))
            event = yield None
            coupled, event = yield from col_scatter(dot_nt(got, upper_coupling[0]), event)
            interior = ((forward - coupled) * row_mask).astype(BF16)
            interior, _ = yield from col_gather(interior, event)
            back = row_scatter(dot_nt(interior, upper_inverse[0])) * col_mask
            return back.reshape(layers, 1, part, col_count), spread

        solved, middles = zip(
            *(
                staggered(chunk(0), chunk(1))
                if chunks == 2
                else [alone(chunk(h)) for h in range(chunks)]
            )
        )
        out = jnp.concatenate(solved, axis=1).reshape(layers * width, col_count).T
        return out[None], jnp.concatenate(middles, axis=0).T

    placed = (
        P("layer", "row", "col"),
        P("layer", "col", "row"),
        P("layer", "row", "col"),
        P("layer", "row", "col"),
        P(("layer", "row"), "col"),
        P("col", ("layer", "row")),
        P("layer", "col", "row"),
        P("col", ("layer", "row")),
        P("layer"),
    )
    return jax.shard_map(
        shards,
        mesh=mesh,
        in_specs=placed,
        out_specs=(P("layer", "col", "row"), P("col", ("layer", "row"))),
        check_vma=False,
    )
```

```python
import jax
import jax.numpy as jnp
from jax import lax
from jax.sharding import PartitionSpec as P

F32 = jnp.float32
BF16 = jnp.bfloat16


def pick(array, index):
    return lax.dynamic_index_in_dim(array, index, 0, keepdims=False)


def place(parts):
    out = jnp.zeros((len(parts),) + parts[0][1].shape, parts[0][1].dtype)
    for index, block in parts:
        out = lax.dynamic_update_index_in_dim(out, block, index, 0)
    return out


WAITS = (1, None, 2, None)


def alone(steps):
    try:
        event = next(steps)
        while True:
            event = steps.send(None)
    except StopIteration as end:
        return end.value


def staggered(first, second):
    ends = {}
    events = {}

    def step(name, chunk, wait=None):
        try:
            events[name] = chunk.send(wait) if name in events else next(chunk)
        except StopIteration as end:
            ends[name] = end.value
            return None
        return events[name]

    step("a", first)
    step("b", second)
    last = None
    for _ in range(4):
        last = step("a", first)
    ahead, behind = ("b", second), ("a", first)
    for stage in range(5):
        seen = [last]
        for wait in WAITS:
            while wait is not None and len(seen) <= wait:
                seen.append(None if behind[0] in ends else step(*behind))
            got = step(*ahead, None if wait is None else seen[wait])
        last = got
        while len(seen) < 6:
            seen.append(None if behind[0] in ends else step(*behind))
        ahead, behind = behind, ahead
    for name, chunk in (("a", first), ("b", second)):
        while name not in ends:
            step(name, chunk)
    return ends["a"], ends["b"]


def dot_nt(a, b):
    return lax.dot_general(a, b, (((1,), (1,)), ((), ())), preferred_element_type=F32)


def solution(mesh):
    layers, rows, cols = (mesh.shape[name] for name in ("layer", "row", "col"))
    pair = 2 if rows % 2 == 0 else 1
    high = rows // pair
    groups = layers * high

    def send_col(block, step):
        return lax.ppermute(block, "col", [(i, i ^ step) for i in range(cols)])

    def send_high(block, step):
        return lax.ppermute(
            block,
            "row",
            [(i, i ^ (step * pair)) for i in range(rows)],
        )

    def send_pair(block):
        return lax.ppermute(block, "row", [(i, i ^ 1) for i in range(rows)])

    def send_group(block, step):
        return lax.ppermute(
            block,
            ("layer", "row"),
            [(i, i ^ (step * pair)) for i in range(layers * rows)],
        )

    def scatter(part, me, size, send):
        total = pick(part, me)
        low = part.astype(BF16)
        got = [send(pick(low, me ^ d), d) for d in range(size - 1, 0, -1)]
        for block in got:
            total = total + block.astype(F32)
        return total

    def gather(block, me, size, send):
        parts = [(me, block)]
        parts += [(me ^ d, send(block, d)) for d in range(size - 1, 0, -1)]
        return place(parts), parts[-1][1]

    def swap_col(block, bits):
        return lax.ppermute(block, "col", [(i, i ^ bits) for i in range(cols)])

    def after(block, event):
        if event is None:
            return block
        row = event.reshape(-1, event.shape[-1])[:1, : block.shape[-1]].astype(F32)
        return block + jnp.where((row < 0) & (row > 0), row, 0).astype(block.dtype)

    def line_scatter(part, me, event):
        low = part.astype(BF16)
        far = swap_col(after(pick(low, me ^ 2), event), 1)
        near = swap_col(after(pick(low, me ^ 1), event), 1)
        event = yield far
        across = pick(part, me ^ 3) + far.astype(F32)
        across = swap_col(after(across, event).astype(BF16), 3)
        event = yield across
        return pick(part, me) + near.astype(F32) + across.astype(F32), event

    def line_gather(block, me, event):
        block = after(block, event)
        across = swap_col(block, 3)
        near = swap_col(block, 1)
        event = yield across
        far = swap_col(after(across, event), 1)
        event = yield far
        return place([(me, block), (me ^ 1, near), (me ^ 3, across), (me ^ 2, far)]), event

    def pair_scatter(part, core):
        if pair == 1:
            return part[:, 0], part
        mine = lax.dynamic_index_in_dim(part, core, 1, keepdims=False)
        other = lax.dynamic_index_in_dim(part, 1 - core, 1, keepdims=False)
        got = send_pair(other.astype(BF16))
        return mine + got.astype(F32), got

    def pair_gather(block, core):
        if pair == 1:
            return block[:, None], block
        got = send_pair(block)
        out = jnp.zeros((block.shape[0], pair) + block.shape[1:], block.dtype)
        out = lax.dynamic_update_index_in_dim(out, block, core, 1)
        return lax.dynamic_update_index_in_dim(out, got, 1 - core, 1), got

    def shards(
        lower_inverse,
        upper_inverse,
        lower_coupling,
        upper_coupling,
        separator_lower,
        separator_upper,
        subtree_rhs,
        separator_rhs,
        column_counts,
    ):
        limit = column_counts[0]
        row_count = lower_inverse.shape[1]
        col_count = lower_inverse.shape[2]
        sep_count, width = separator_rhs.shape
        chunks = 2 if width % 32 == 0 else 1
        part = width // chunks
        total = layers * rows * part
        layer, row, col = (lax.axis_index(name) for name in ("layer", "row", "col"))
        core, up = row % pair, row // pair
        group = layer * high + up
        col_mask = (col * col_count + lax.iota(jnp.int32, col_count) < limit).astype(F32)
        row_mask = (row * row_count + lax.iota(jnp.int32, row_count) < limit).astype(F32)

        def col_scatter(x, event):
            pieces = x.reshape(cols, -1, x.shape[1])
            if cols == 4:
                return (yield from line_scatter(pieces, col, event))
            return scatter(pieces, col, cols, send_col), None

        def col_gather(x, event):
            if cols == 4:
                out, event = yield from line_gather(x, col, event)
            else:
                out = gather(x, col, cols, send_col)[0]
            return out.reshape(total, -1), event

        def all_scatter(x):
            n = x.shape[1]
            mine, got = pair_scatter(x.reshape(groups, pair, part, n), core)
            yield got
            out = scatter(mine, group, groups, send_group)
            yield out
            return out

        def all_gather(x):
            mine, got = gather(x, group, groups, send_group)
            yield got
            out, got = pair_gather(mine, core)
            yield got
            return out.reshape(total, -1)

        def row_gather(x):
            mine = gather(x, up, high, send_high)[0]
            return pair_gather(mine, core)[0].reshape(total, -1)

        def row_scatter(x):
            n = x.shape[1]
            mine = pair_scatter(x.reshape(high, pair, -1, n), core)[0]
            return scatter(mine, up, high, send_high)

        given = (subtree_rhs[0] * col_mask[:, None]).astype(BF16).T
        given = given.reshape(layers, chunks, part, col_count)
        sep_given = separator_rhs.T.reshape(chunks, part, sep_count)

        def chunk(h):
            masked = row_gather(given[:, h].reshape(layers * part, col_count))
            event = yield None
            forward, event = yield from col_scatter(dot_nt(masked, lower_inverse[0]), event)
            forward = lax.optimization_barrier(forward * row_mask)
            low, _ = yield from col_gather(forward.astype(BF16), event)
            update = jnp.dot(low, lower_coupling[0], preferred_element_type=F32)
            share = yield from all_scatter(update)
            reduced = yield from all_gather((sep_given[h] - share).astype(BF16))
            event = yield None
            middle, event = yield from col_scatter(dot_nt(reduced, separator_lower), event)
            middle, _ = yield from col_gather(middle.astype(BF16), event)
            spread = yield from all_scatter(dot_nt(middle, separator_upper))
            got = yield from all_gather(spread.astype(BF16))
            event = yield None
            coupled, event = yield from col_scatter(dot_nt(got, upper_coupling[0]), event)
            interior = ((forward - coupled) * row_mask).astype(BF16)
            interior, _ = yield from col_gather(interior, event)
            back = row_scatter(dot_nt(interior, upper_inverse[0])) * col_mask
            return back.reshape(layers, 1, part, col_count), spread

        solved, middles = zip(
            *(
                staggered(chunk(0), chunk(1))
                if chunks == 2
                else [alone(chunk(h)) for h in range(chunks)]
            )
        )
        out = jnp.concatenate(solved, axis=1).reshape(layers * width, col_count).T
        return out[None], jnp.concatenate(middles, axis=0).T

    placed = (
        P("layer", "row", "col"),
        P("layer", "col", "row"),
        P("layer", "row", "col"),
        P("layer", "row", "col"),
        P(("layer", "row"), "col"),
        P("col", ("layer", "row")),
        P("layer", "col", "row"),
        P("col", ("layer", "row")),
        P("layer"),
    )
    return jax.shard_map(
        shards,
        mesh=mesh,
        in_specs=placed,
        out_specs=(P("layer", "col", "row"), P("col", ("layer", "row"))),
        check_vma=False,
    )
```
